512 devices in a mesh: head: 8 (over z_lo), blk: 32 (over z_hi, x, y), enc: 2 (over core).
Axes of the slice: x: 4, y: 4, z: 16 (z_hi: 2, z_lo: 8; z = z_hi * 8 + z_lo), core: 2. Of those that a mesh axis runs over, the one named last changes fastest.
Arguments:
- queries: bfloat16 [32, 896, 5120], P('blk', ('head', 'enc')), may hold values from -30 to 30
- key_rows: bfloat16 [32, 896, 5120], P('blk', ('head', 'enc')), may hold values from -30 to 30
- value_rows: bfloat16 [32, 896, 5120], P('blk', ('head', 'enc')), may hold values from -6 to 6
- text_queries: bfloat16 [32, 896, 5120], P('blk', ('head', 'enc')), may hold values from -300 to 300
- prompt_embed: bfloat16 [512, 4096], P('enc', 'blk'), may hold values from -6 to 6
- key_weight: bfloat16 [4096, 5120], P('blk', 'head'), may hold values from -0.09375 to 0.09375
- value_weight: bfloat16 [4096, 5120], P('blk', 'head'), may hold values from -0.09375 to 0.09375
- stop_count: int32 [32], P('blk'), may hold values from 1 to 3, as said below
- prompt_length: int32 [1], replicated, may hold values from 64 to 512
Outputs:
- mixed: bfloat16 [32, 896, 5120], P('blk', ('head', 'enc'))
The draws below stay inside these ranges and needn't reach their ends.
Inputs may be any that keep to these rules, and one draw needn't show every extreme that they name: `stop_count`: some block sees all 3 blocks.
All inputs are finite; a program needn't handle non-finite values.
Results may differ from the reference program's by a relative error of at most 0.0083.
Values may be sent and summed in bfloat16 or wider, within the bound.
A program may use at most 64 MiB of HBM per device.

```python
import jax
import jax.numpy as jnp
from jax import lax

HEADS = 40
HEAD_DIM = 128
D = 5120
DT = 4096
TEXT = 512
TB = 896
STOPS = 3
BLOCKS = 32


def draw_queries(key, part):
    key = jax.random.fold_in(key, 3)
    result = 2.5 * jax.random.truncated_normal(key, -6.0, 6.0, (BLOCKS, TB, D), jnp.float32)
    return result.astype(jnp.bfloat16)


def draw_key_rows(key, part):
    key = jax.random.fold_in(key, 4)
    result = jax.random.truncated_normal(key, -6.0, 6.0, (BLOCKS, TB, D), jnp.float32)
    return result.astype(jnp.bfloat16)


def draw_text_queries(key, part):
    key = jax.random.fold_in(key, 7)
    result = 2.5 * jax.random.truncated_normal(key, -6.0, 6.0, (BLOCKS, TB, D), jnp.float32)
    return result.astype(jnp.bfloat16)


def draw_stop_count(key, part):
    key = jax.random.fold_in(key, 5)
    first_key, second_key = jax.random.split(key)
    counts = jax.random.randint(first_key, (BLOCKS,), 1, STOPS + 1, dtype=jnp.int32)
    spot = jax.random.randint(second_key, (), 0, BLOCKS, dtype=jnp.int32)
    return jnp.where(jnp.arange(BLOCKS, dtype=jnp.int32) == spot, jnp.int32(STOPS), counts)


def level_of(stream_key, extent, pieces, smallest, largest):
    def one(axis_at, parts):
        heights = jax.random.uniform(jax.random.fold_in(jax.random.fold_in(stream_key, 6), axis_at), (parts,), jnp.float32, smallest / len(pieces), largest / len(pieces))
        return jnp.repeat(jnp.exp(heights), extent[axis_at] // parts).reshape((-1,) + (1,) * (len(extent) - axis_at - 1))

    loudness = one(*pieces[0])
    for cut in pieces[1:]:
        loudness = loudness * one(*cut)
    return loudness


def gaussian(stream_key, shape, spread, most, pieces=(), held_as=jnp.bfloat16):
    factor_of = level_of(stream_key, shape, pieces, -0.22, 0.18) if pieces else 1.0
    values = jax.random.normal(stream_key, shape, jnp.float32) * spread * factor_of
    return jnp.minimum(jnp.maximum(values, -most), most).astype(held_as)


def setup_inputs(seed: int = 0) -> dict:
    streams_of = jax.random.split(jax.random.key(seed), 10)
    queries = draw_queries(jax.random.fold_in(streams_of[9], 71), 0)
    key_rows = draw_key_rows(jax.random.fold_in(streams_of[9], 71), 0)
    value_rows = gaussian(streams_of[2], (BLOCKS, TB, D), 1.0, 6.0, ((0, 32), (1, 16)))
    text_queries = draw_text_queries(jax.random.fold_in(streams_of[9], 71), 0)
    prompt_embed = gaussian(streams_of[4], (TEXT, DT), 1.0, 6.0, ((0, 2), (1, 32)))
    key_weight = gaussian(streams_of[5], (DT, D), DT ** -0.5, 0.09375, ((0, 32), (1, 8)))
    value_weight = gaussian(streams_of[6], (DT, D), DT ** -0.5, 0.09375, ((0, 32), (1, 8)))
    stop_count = draw_stop_count(jax.random.fold_in(streams_of[9], 71), 0)
    prompt_length = jax.random.randint(streams_of[8], (1,), TEXT // 8, TEXT + 1).astype(jnp.int32)
    return {"queries": queries, "key_rows": key_rows, "value_rows": value_rows, "text_queries": text_queries, "prompt_embed": prompt_embed, "key_weight": key_weight, "value_weight": value_weight, "stop_count": stop_count, "prompt_length": prompt_length}


def head_attention(head_query, known_keys, known_values, allowed):
    scores = jnp.dot(head_query.astype(jnp.float32), known_keys.astype(jnp.float32).T) * (float(HEAD_DIM) ** -0.5)
    scores = jnp.where(allowed[None, :], scores, jnp.float32(-1e30))
    row_peak = jnp.max(scores, axis=1, keepdims=True)
    weights = jnp.where(allowed[None, :], jnp.exp(scores - row_peak), jnp.float32(0.0))
    weight_sum = jnp.sum(weights, axis=1, keepdims=True)
    rounded = weights.astype(jnp.bfloat16)
    return jnp.dot(rounded.astype(jnp.float32), known_values.astype(jnp.float32)) / weight_sum


def by_heads(matrix):
    return jnp.transpose(matrix.reshape(matrix.shape[0], HEADS, HEAD_DIM), (1, 0, 2))


def reference(queries, key_rows, value_rows, text_queries, prompt_embed, key_weight, value_weight, stop_count, prompt_length):
    text_keys = jnp.dot(prompt_embed, key_weight, preferred_element_type=jnp.float32).astype(jnp.bfloat16)
    text_values = jnp.dot(prompt_embed, value_weight, preferred_element_type=jnp.float32).astype(jnp.bfloat16)
    text_live = jnp.arange(TEXT, dtype=jnp.int32) < prompt_length[0]

    def one_block(block_index):
        seen_keys = []
        seen_values = []
        allowed_parts = []
        for offset in range(STOPS):
            source = ((block_index - offset) % BLOCKS).astype(jnp.int32)
            seen_keys.append(lax.dynamic_index_in_dim(key_rows, source, 0, keepdims=False))
            seen_values.append(lax.dynamic_index_in_dim(value_rows, source, 0, keepdims=False))
            allowed_parts.append(jnp.full((TB,), offset, jnp.int32) < stop_count[block_index])
        near_keys = jnp.concatenate(seen_keys, axis=0)
        near_values = jnp.concatenate(seen_values, axis=0)
        allowed = jnp.concatenate(allowed_parts, axis=0)

        def one_head(items):
            head_query, head_keys, head_values, head_cross, cross_keys, cross_values = items
            self_out = head_attention(head_query, head_keys, head_values, allowed)
            cross_out = head_attention(head_cross, cross_keys, cross_values, text_live)
            return (self_out + cross_out).astype(jnp.bfloat16)

        result = lax.map(one_head, (by_heads(queries[block_index]), by_heads(near_keys), by_heads(near_values), by_heads(text_queries[block_index]), by_heads(text_keys), by_heads(text_values)))
        return jnp.transpose(result, (1, 0, 2)).reshape(TB, HEADS * HEAD_DIM)

    return lax.map(one_block, jnp.arange(BLOCKS, dtype=jnp.int32))
```

```python
import functools

import jax
import jax.numpy as jnp
from jax import lax
from jax.experimental import pallas as pl
from jax.experimental.pallas import tpu as pltpu
from jax.sharding import PartitionSpec as P

HEAD_DIM = 128
STOPS = 3
MESH = pl.DeviceIdType.MESH
COLUMNS = 16
RING = 16
SOURCES = 16
SLOTS = 3
SCORE = float(HEAD_DIM) ** -0.5 * 1.4426950408889634
OUT = 1.0e30


def kernel(
    q_ref, k_ref, v_ref, tq_ref, emb_ref, wk_ref, wv_ref, stop_ref, plen_ref, out_ref,
    kv_in, q_in, kv, part, part_in, total, other, text, result, stops,
    kv_recv, q_recv, send, fwd_send, fwd_recv, o_send, o_recv, t_send, t_recv,
):
    g = lax.axis_index("head")
    b = lax.axis_index("blk")
    e = lax.axis_index("enc")
    p = b // COLUMNS
    c = b % COLUMNS
    z = p * 8 + g
    wide = p == g % 2
    home = e == p
    my_col = g * 640 + jnp.where(wide, 0, 384)
    slot = g * 2 + e
    tokens = kv_in.shape[3]
    rows = SOURCES * tokens

    barrier = pltpu.get_barrier_semaphore()

    def greet(device):
        pl.semaphore_signal(barrier, inc=1, device_id=device, device_id_type=MESH)

    def greet_z(n, _):
        tg, tp = n % 8, n // 8

        @pl.when(jnp.logical_or(n != z, jnp.logical_not(home)))
        def _():
            greet((tg, tp * COLUMNS + c, p))

        return 0

    def greet_givers(n, _):
        greet((n, e * COLUMNS + c, 1 - p))
        return 0

    def greet_plane(n, _):
        greet((g, p * COLUMNS + (c + n // 2) % COLUMNS, n % 2))
        return 0

    lax.fori_loop(0, RING, greet_z, 0)
    lax.fori_loop(0, 8, greet_givers, 0)
    lax.fori_loop(2, 2 * COLUMNS, greet_plane, 0)

    @pl.when(home)
    def _():
        pl.semaphore_wait(barrier, 53)

    @pl.when(jnp.logical_not(home))
    def _():
        pl.semaphore_wait(barrier, 54)

    def send_heads(hs, refs, landing, recv, sends):
        def one(n, _):
            m = RING - 1 - n
            t = (z + ((m + 1) // 2) * (2 * (m % 2) - 1) + RING) % RING
            tg, tp = t % 8, t // 8
            t_wide = tp == tg % 2
            col = pl.multiple_of(tg * 640 + jnp.where(t_wide, 0, 384) + hs * HEAD_DIM, HEAD_DIM)
            mine = jnp.logical_and(t == z, home)
            needed = t_wide if hs == 2 else True

            @pl.when(jnp.logical_and(jnp.logical_not(mine), needed))
            def _():
                for i, ref in enumerate(refs):
                    pltpu.make_async_remote_copy(
                        src_ref=ref.at[:, pl.ds(col, HEAD_DIM)],
                        dst_ref=landing.at[hs, i, slot],
                        send_sem=send.at[sends + i],
                        recv_sem=recv.at[hs],
                        device_id=(tg, tp * COLUMNS + c, p),
                        device_id_type=MESH,
                    ).start()

            @pl.when(jnp.logical_and(mine, needed))
            def _():
                for i, ref in enumerate(refs):
                    pltpu.make_async_copy(
                        ref.at[:, pl.ds(col, HEAD_DIM)], landing.at[hs, i, slot], recv.at[hs]
                    ).start()

            return 0

        lax.fori_loop(0, RING, one, 0)

    def wait_for(ref, sem):
        pltpu.make_async_copy(ref, ref, sem).wait()

    def per_slot(hs, run):
        if hs == 2:
            pl.when(wide)(run)
        else:
            run()

    def forward(hs, m):
        next_c = (c + 1) % COLUMNS
        next_e = jnp.where(c == COLUMNS - 1, 1 - e, e)
        return pltpu.make_async_remote_copy(
            src_ref=kv.at[m, hs],
            dst_ref=kv.at[m + 1, hs],
            send_sem=fwd_send.at[m, hs],
            recv_sem=fwd_recv.at[m, hs],
            device_id=(g, p * COLUMNS + next_c, next_e),
            device_id_type=MESH,
        )

    def keys_arrive(hs):
        def run():
            wait_for(kv_in.at[hs], kv_recv.at[hs])
            for i in range(2):
                whole = kv_in[hs, i].astype(jnp.float32).reshape(rows, HEAD_DIM)
                kv[0, hs, i] = whole.astype(jnp.bfloat16)
            forward(hs, 0).start()

        per_slot(hs, run)

    def keys_pass(hs):
        def run():
            forward(hs, 0).wait_recv()
            forward(hs, 1).start()

        per_slot(hs, run)

    send_heads(0, (k_ref, v_ref), kv_in, kv_recv, 0)

    stops[0] = jnp.full((8, 128), stop_ref[0].astype(jnp.float32))
    trade = pltpu.make_async_remote_copy(
        src_ref=stops.at[0],
        dst_ref=stops.at[1],
        send_sem=t_send.at[3],
        recv_sem=t_recv.at[3],
        device_id=(g, (1 - p) * COLUMNS + c, e),
        device_id_type=MESH,
    )
    trade.start()

    for i, w_ref in enumerate((wk_ref, wv_ref)):
        product = jnp.dot(emb_ref[...], w_ref[...], preferred_element_type=jnp.float32)
        part[:, i] = product.reshape(part.shape[0], part.shape[2], part.shape[3])

    def send_part(n, _):
        cc = (c + n) % COLUMNS
        pltpu.make_async_remote_copy(
            src_ref=part.at[cc],
            dst_ref=part_in.at[c],
            send_sem=t_send.at[0],
            recv_sem=t_recv.at[0],
            device_id=(g, p * COLUMNS + cc, e),
            device_id_type=MESH,
        ).start()
        return 0

    lax.fori_loop(1, COLUMNS, send_part, 0)
    part_in[c] = part[c]

    send_heads(1, (k_ref, v_ref), kv_in, kv_recv, 0)
    keys_arrive(0)
    send_heads(2, (k_ref, v_ref), kv_in, kv_recv, 0)

    wait_for(part_in.at[pl.ds(0, COLUMNS - 1)], t_recv.at[0])
    total[...] = jnp.sum(part_in[...], axis=0)

    def swap(left):
        cols = (384, 256) if left else (0, 384)
        return pltpu.make_async_remote_copy(
            src_ref=total.at[:, :, pl.ds(*cols)],
            dst_ref=other.at[:, :, pl.ds(0, cols[1])],
            send_sem=t_send.at[1],
            recv_sem=t_recv.at[1],
            device_id=(g, (1 - p) * COLUMNS + c, e),
            device_id_type=MESH,
        )

    @pl.when(wide)
    def _():
        swap(True).start()

    @pl.when(jnp.logical_not(wide))
    def _():
        swap(False).start()

    keys_arrive(1)
    send_heads(0, (q_ref, tq_ref), q_in, q_recv, 2)
    keys_pass(0)

    chunk = e * COLUMNS + c

    @pl.when(wide)
    def _():
        swap(False).wait_recv()
        text[chunk] = (total[:, :, 0:384] + other[...]).astype(jnp.bfloat16)

    @pl.when(jnp.logical_not(wide))
    def _():
        swap(True).wait_recv()
        both = (total[:, :, 384:640] + other[:, :, 0:256]).astype(jnp.bfloat16)
        text[chunk, :, :, 0:256] = both
        text[chunk, :, :, 256:384] = jnp.zeros((2, 16, 128), jnp.bfloat16)

    def send_text(n, _):
        pltpu.make_async_remote_copy(
            src_ref=text.at[chunk],
            dst_ref=text.at[chunk],
            send_sem=t_send.at[2],
            recv_sem=t_recv.at[2],
            device_id=(g, p * COLUMNS + (c + n // 2) % COLUMNS, (e + n) % 2),
            device_id_type=MESH,
        ).start()
        return 0

    lax.fori_loop(1, 2 * COLUMNS, send_text, 0)

    keys_arrive(2)
    send_heads(1, (q_ref, tq_ref), q_in, q_recv, 2)
    keys_pass(1)
    send_heads(2, (q_ref, tq_ref), q_in, q_recv, 2)
    keys_pass(2)
    wait_for(text.at[pl.ds(0, 2 * COLUMNS - 1)], t_recv.at[2])

    group = 4
    trade.wait()
    here = jnp.where(home, 1.0, 0.0)
    stop = stops[0, 0:1, 0:1] * here + stops[1, 0:1, 0:1] * (1.0 - here)
    shut = [jnp.where(m < stop, 0.0, OUT) for m in range(STOPS)]
    live = lax.broadcasted_iota(jnp.int32, (1, 2 * COLUMNS * 16), 1) < plen_ref[0]

    def attend(hs):
        def block(i, _):
            query, cross = (
                q_in[hs, j, pl.ds(i * group, group)].astype(jnp.float32).reshape(group * tokens, HEAD_DIM).astype(jnp.bfloat16)
                for j in range(2)
            )
            scores = [
                lax.dot_general(query, kv[m, hs, 0], (((1,), (1,)), ((), ())), preferred_element_type=jnp.float32)
                for m in range(STOPS)
            ]
            peaks = [jnp.max(s, axis=1, keepdims=True) - shut[m] for m, s in enumerate(scores)]
            peak = jnp.maximum(jnp.maximum(peaks[0], peaks[1]), peaks[2]) * SCORE
            weights = [jnp.exp2(s * SCORE - (peak + shut[m])) for m, s in enumerate(scores)]
            sums = sum(jnp.sum(w, axis=1, keepdims=True) for w in weights)
            mix = sum(
                jnp.dot(w.astype(jnp.bfloat16), kv[m, hs, 1], preferred_element_type=jnp.float32)
                for m, w in enumerate(weights)
            )
            text_keys = text[:, 0, :, hs * 128 : hs * 128 + 128].reshape(512, HEAD_DIM)
            text_values = text[:, 1, :, hs * 128 : hs * 128 + 128].reshape(512, HEAD_DIM)
            scores = lax.dot_general(cross, text_keys, (((1,), (1,)), ((), ())), preferred_element_type=jnp.float32)
            scores = jnp.where(live, scores, -OUT)
            weights = jnp.exp2((scores - jnp.max(scores, axis=1, keepdims=True)) * SCORE)
            cross_mix = jnp.dot(weights.astype(jnp.bfloat16), text_values, preferred_element_type=jnp.float32)
            mixed = mix / sums + cross_mix / jnp.sum(weights, axis=1, keepdims=True)
            result[hs, pl.ds(i * group, group)] = mixed.reshape(group, tokens, HEAD_DIM).astype(jnp.bfloat16)

            def give(n, _):
                s = i * group + n
                mine = jnp.logical_and(s == slot, home)
                where = out_ref.at[:, pl.ds(pl.multiple_of(my_col + hs * HEAD_DIM, HEAD_DIM), HEAD_DIM)]

                @pl.when(jnp.logical_not(mine))
                def _():
                    pltpu.make_async_remote_copy(
                        src_ref=result.at[hs, s],
                        dst_ref=where,
                        send_sem=o_send.at[hs],
                        recv_sem=o_recv,
                        device_id=(s // 2, e * COLUMNS + c, s % 2),
                        device_id_type=MESH,
                    ).start()

                @pl.when(mine)
                def _():
                    pltpu.make_async_copy(result.at[hs, s], where, o_recv).start()

                return 0

            lax.fori_loop(0, group, give, 0)
            return 0

        def run():
            wait_for(q_in.at[hs], q_recv.at[hs])
            forward(hs, 1).wait_recv()
            lax.fori_loop(0, SOURCES // group, block, 0)

        per_slot(hs, run)

    for hs in range(SLOTS):
        attend(hs)

    def token_sends(width):
        for i, ref in enumerate((k_ref, v_ref, q_ref, tq_ref)):
            wait_for(ref.at[:, pl.ds(0, width * HEAD_DIM)], send.at[i])

    @pl.when(jnp.logical_not(home))
    def _():
        token_sends(40)

    @pl.when(jnp.logical_and(home, wide))
    def _():
        token_sends(37)

    @pl.when(jnp.logical_and(home, jnp.logical_not(wide)))
    def _():
        token_sends(38)

    wait_for(part.at[pl.ds(0, COLUMNS - 1)], t_send.at[0])

    @pl.when(wide)
    def _():
        swap(True).wait_send()

    @pl.when(jnp.logical_not(wide))
    def _():
        swap(False).wait_send()

    wait_for(text.at[pl.ds(0, 2 * COLUMNS - 1)], t_send.at[2])
    for hs in range(SLOTS):

        def finish(hs=hs):
            forward(hs, 0).wait_send()
            forward(hs, 1).wait_send()

            @pl.when(home)
            def _():
                wait_for(result.at[hs, pl.ds(0, SOURCES - 1)], o_send.at[hs])

            @pl.when(jnp.logical_not(home))
            def _():
                wait_for(result.at[hs], o_send.at[hs])

        per_slot(hs, finish)
    wait_for(out_ref, o_recv)


def body(
    queries,
    key_rows,
    value_rows,
    text_queries,
    prompt_embed,
    key_weight,
    value_weight,
    stop_count,
    prompt_length,
):
    tokens, width = queries.shape[1:]
    heads_here = key_weight.shape[1]
    text_rows = prompt_embed.shape[0] // COLUMNS
    dma = pltpu.SemaphoreType.DMA
    mixed = pl.pallas_call(
        kernel,
        out_shape=jax.ShapeDtypeStruct((tokens, width), jnp.bfloat16),
        in_specs=[pl.BlockSpec(memory_space=pl.ANY)] * 4
        + [pl.BlockSpec(memory_space=pltpu.VMEM)] * 3
        + [pl.BlockSpec(memory_space=pltpu.SMEM)] * 2,
        out_specs=pl.BlockSpec(memory_space=pl.ANY),
        scratch_shapes=[
            pltpu.VMEM((SLOTS, 2, SOURCES, tokens, HEAD_DIM), jnp.bfloat16),
            pltpu.VMEM((SLOTS, 2, SOURCES, tokens, HEAD_DIM), jnp.bfloat16),
            pltpu.VMEM((STOPS, SLOTS, 2, SOURCES * tokens, HEAD_DIM), jnp.bfloat16),
            pltpu.VMEM((COLUMNS, 2, text_rows, heads_here), jnp.float32),
            pltpu.VMEM((COLUMNS, 2, text_rows, heads_here), jnp.float32),
            pltpu.VMEM((2, text_rows, heads_here), jnp.float32),
            pltpu.VMEM((2, text_rows, SLOTS * HEAD_DIM), jnp.float32),
            pltpu.VMEM((2 * COLUMNS, 2, text_rows, SLOTS * HEAD_DIM), jnp.bfloat16),
            pltpu.VMEM((SLOTS, SOURCES, tokens, HEAD_DIM), jnp.bfloat16),
            pltpu.VMEM((2, 8, 128), jnp.float32),
            dma((SLOTS,)),
            dma((SLOTS,)),
            dma((4,)),
            dma((2, SLOTS)),
            dma((2, SLOTS)),
            dma((SLOTS,)),
            dma,
            dma((4,)),
            dma((4,)),
        ],
        compiler_params=pltpu.CompilerParams(
            collective_id=0, has_side_effects=True, vmem_limit_bytes=48 * 1024 * 1024
        ),
    )(
        queries[0],
        key_rows[0],
        value_rows[0],
        text_queries[0],
        prompt_embed,
        key_weight,
        value_weight,
        stop_count,
        prompt_length,
    )
    return mixed[None]


def solution(mesh):
    placed = (
        P("blk", ("head", "enc"), None),
        P("blk", ("head", "enc"), None),
        P("blk", ("head", "enc"), None),
        P("blk", ("head", "enc"), None),
        P("enc", "blk"),
        P("blk", "head"),
        P("blk", "head"),
        P("blk"),
        P(),
    )
    return jax.shard_map(
        body, mesh=mesh, in_specs=placed, out_specs=P("blk", ("head", "enc"), None), check_vma=False
    )
```

```python
import functools

import jax
import jax.numpy as jnp
from jax import lax
from jax.experimental import pallas as pl
from jax.experimental.pallas import tpu as pltpu
from jax.sharding import PartitionSpec as P

HEAD_DIM = 128
STOPS = 3
MESH = pl.DeviceIdType.MESH
COLUMNS = 16
RING = 16
SOURCES = 16
SLOTS = 3
SCORE = float(HEAD_DIM) ** -0.5 * 1.4426950408889634
OUT = 1.0e30
TRADE, PART, SWAP, ASK, UP, ROWS, ANSWER = range(7)


def kernel(
    q_ref, k_ref, v_ref, tq_ref, emb_hbm, wk_hbm, wv_hbm, stop_ref, plen_ref, out_ref,
    kv_in, q_in, kv, part, part_in, total, other, piece, column, text, result, stops, emb_ref, wk_ref, wv_ref,
    cross_in, cross_out, self_mix, cross_mix,
    kv_recv, q_recv, send, fwd_send, fwd_recv, o_send, o_recv, t_send, t_recv, w_sem,
):
    g = lax.axis_index("head")
    b = lax.axis_index("blk")
    e = lax.axis_index("enc")
    p = b // COLUMNS
    c = b % COLUMNS
    x, y = c // 4, c % 4
    z = p * 8 + g
    wide = z % 2 == 0
    home = e == p
    my_col = (z // 2) * 640 + jnp.where(wide, 0, 384)
    slot = g * 2 + e
    tokens = kv_in.shape[3]
    rows = SOURCES * tokens

    weights = [
        pltpu.make_async_copy(source, place, w_sem.at[i])
        for i, (source, place) in enumerate(((emb_hbm, emb_ref), (wk_hbm, wk_ref), (wv_hbm, wv_ref)))
    ]
    for copy in weights:
        copy.start()

    barrier = pltpu.get_barrier_semaphore()

    def greet(device):
        pl.semaphore_signal(barrier, inc=1, device_id=device, device_id_type=MESH)

    def at(height, core):
        return (height % 8, (height // 8) * COLUMNS + c, core)

    def beside(where, core):
        return (g, p * COLUMNS + where, core)

    def greet_column(n, _):
        height, core = n // 2, n % 2

        @pl.when(jnp.logical_or(height != z, core != e))
        def _():
            greet(at(height, core))

        return 0

    def greet_plane(n, _):
        greet(beside((c + n // 2) % COLUMNS, n % 2))
        return 0

    lax.fori_loop(0, 2 * RING, greet_column, 0)
    lax.fori_loop(2, 2 * COLUMNS, greet_plane, 0)
    pl.semaphore_wait(barrier, 61)

    def copy_to(source, place, kind, device):
        return pltpu.make_async_remote_copy(
            src_ref=source,
            dst_ref=place,
            send_sem=t_send.at[kind],
            recv_sem=t_recv.at[kind],
            device_id=device,
            device_id_type=MESH,
        )

    def give(mine, source, place, kind, device):
        @pl.when(jnp.logical_not(mine))
        def _():
            copy_to(source, place, kind, device).start()

        @pl.when(mine)
        def _():
            pltpu.make_async_copy(source, place, t_recv.at[kind]).start()

    def send_heads(kind, hs, half):
        refs, landing, recv = ((k_ref, v_ref), kv_in, kv_recv) if kind == 0 else ((q_ref,), q_in, q_recv)

        def one(n, _):
            m = jnp.where(n % 2 == 0, RING - 1 - n // 2, n // 2)
            t = (z + ((m + 1) // 2) * (2 * (m % 2) - 1) + RING) % RING
            col = pl.multiple_of((t // 2) * 640 + (t % 2) * 384 + hs * HEAD_DIM, HEAD_DIM)
            mine = jnp.logical_and(t == z, home)
            needed = t % 2 == 0 if hs == 2 else True

            @pl.when(jnp.logical_and(jnp.logical_not(mine), needed))
            def _():
                for i, ref in enumerate(refs):
                    pltpu.make_async_remote_copy(
                        src_ref=ref.at[:, pl.ds(col, HEAD_DIM)],
                        dst_ref=landing.at[hs, i, slot],
                        send_sem=send.at[kind, hs, half],
                        recv_sem=recv.at[hs],
                        device_id=at(t, p),
                        device_id_type=MESH,
                    ).start()

            @pl.when(jnp.logical_and(mine, needed))
            def _():
                for i, ref in enumerate(refs):
                    pltpu.make_async_copy(
                        ref.at[:, pl.ds(col, HEAD_DIM)], landing.at[hs, i, slot], recv.at[hs]
                    ).start()

            return 0

        lax.fori_loop(8 * half, 8 * half + 8, one, 0)

    def sent(kind, hs, half):
        landing = kv_in if kind == 0 else q_in
        count = 4 if hs == 2 else 8

        def left(copies):
            wait_for(landing.at[hs, :, pl.ds(0, copies)], send.at[kind, hs, half])

        if half == 1:
            left(count)
            return
        keeps = jnp.logical_and(home, wide) if hs == 2 else home

        @pl.when(keeps)
        def _():
            left(count - 1)

        @pl.when(jnp.logical_not(keeps))
        def _():
            left(count)

    def wait_for(ref, sem):
        pltpu.make_async_copy(ref, ref, sem).wait()

    def per_slot(hs, run):
        if hs == 2:
            pl.when(wide)(run)
        else:
            run()

    def forward(hs, m):
        next_c = (c + 1) % COLUMNS
        next_e = jnp.where(c == COLUMNS - 1, 1 - e, e)
        return pltpu.make_async_remote_copy(
            src_ref=kv.at[m, hs],
            dst_ref=kv.at[m + 1, hs],
            send_sem=fwd_send.at[m, hs],
            recv_sem=fwd_recv.at[m, hs],
            device_id=(g, p * COLUMNS + next_c, next_e),
            device_id_type=MESH,
        )

    def keys_arrive(hs):
        def run():
            wait_for(kv_in.at[hs], kv_recv.at[hs])
            for i in range(2):
                whole = kv_in[hs, i].astype(jnp.float32).reshape(rows, HEAD_DIM)
                kv[0, hs, i] = whole.astype(jnp.bfloat16)
            forward(hs, 0).start()

        per_slot(hs, run)

    def keys_pass(hs):
        def run():
            forward(hs, 0).wait_recv()
            forward(hs, 1).start()

        per_slot(hs, run)


    send_heads(0, 0, 0)
    send_heads(0, 0, 1)

    stops[0] = jnp.full((8, 128), stop_ref[0].astype(jnp.float32))
    trade = copy_to(stops.at[0], stops.at[1], TRADE, at((1 - p) * 8 + g, e))
    trade.start()

    for copy in weights:
        copy.wait()

    for i, w_ref in enumerate((wk_ref, wv_ref)):
        product = jnp.dot(emb_ref[...], w_ref[...], preferred_element_type=jnp.float32)
        part[:, i] = product.reshape(part.shape[0], part.shape[2], part.shape[3])

    def send_part(n, _):
        cc = (c + n) % COLUMNS
        copy_to(part.at[cc], part_in.at[c], PART, beside(cc, e)).start()
        return 0

    lax.fori_loop(1, COLUMNS, send_part, 0)
    part_in[c] = part[c]

    lot = 5 * HEAD_DIM
    mine5 = 2 * x + e

    def send_cross(n, _):
        to = (mine5 + n) % 8
        source = tq_ref.at[:, pl.ds(pl.multiple_of(to * lot, HEAD_DIM), lot)]
        give(n == 0, source, cross_in.at[mine5], ASK, beside((to // 2) * 4 + y, to % 2))
        return 0

    lax.fori_loop(0, 8, send_cross, 0)

    sent(0, 0, 0)
    send_heads(0, 1, 0)
    sent(0, 0, 1)
    send_heads(0, 1, 1)
    keys_arrive(0)

    wait_for(part_in.at[pl.ds(0, COLUMNS - 1)], t_recv.at[PART])
    total[...] = jnp.sum(part_in[...], axis=0)
    for n in range(5):
        cols = pl.ds(n * HEAD_DIM, HEAD_DIM)
        copy_to(total.at[1 - p, :, cols], other.at[:, cols], SWAP, at((1 - p) * 8 + g, e)).start()

    sent(0, 1, 0)
    send_heads(0, 2, 0)
    send_heads(0, 2, 1)
    keys_pass(0)

    wait_for(other, t_recv.at[SWAP])
    piece[...] = (total[p] + other[...]).astype(jnp.bfloat16)
    column[p, g] = piece[...]

    def send_up(n, _):
        copy_to(piece, column.at[p, g], UP, at((z + n) % RING, e)).start()
        return 0

    lax.fori_loop(1, RING, send_up, 0)

    sent(0, 1, 1)
    send_heads(1, 0, 0)
    send_heads(1, 0, 1)
    keys_arrive(1)

    sent(0, 2, 0)
    sent(0, 2, 1)
    send_heads(1, 1, 0)
    send_heads(1, 1, 1)
    keys_arrive(2)
    keys_pass(1)

    sent(1, 0, 0)
    sent(1, 0, 1)
    send_heads(1, 2, 0)
    send_heads(1, 2, 1)
    keys_pass(2)

    group = 4
    trade.wait()
    here = jnp.where(home, 1.0, 0.0)
    stop = stops[0, 0:1, 0:1] * here + stops[1, 0:1, 0:1] * (1.0 - here)
    shut = [jnp.where(m < stop, 0.0, OUT) for m in range(STOPS)]
    at_row = lax.broadcasted_iota(jnp.int32, (1, 2 * COLUMNS * 16), 1)
    live = at_row < plen_ref[0]

    def flat(values):
        return values.astype(jnp.float32).reshape(-1, HEAD_DIM).astype(jnp.bfloat16)

    def cross():
        def head(h, _):
            cols = pl.ds(pl.multiple_of(h * HEAD_DIM, HEAD_DIM), HEAD_DIM)
            query = flat(cross_in[:, :, cols])
            text_keys = text[:, 0, :, cols].reshape(512, HEAD_DIM)
            text_values = text[:, 1, :, cols].reshape(512, HEAD_DIM)
            scores = lax.dot_general(query, text_keys, (((1,), (1,)), ((), ())), preferred_element_type=jnp.float32)
            scores = jnp.where(live, scores, -OUT)
            weights = jnp.exp2((scores - jnp.max(scores, axis=1, keepdims=True)) * SCORE)
            mix = jnp.dot(weights.astype(jnp.bfloat16), text_values, preferred_element_type=jnp.float32)
            mix = mix / jnp.sum(weights, axis=1, keepdims=True)
            cross_out[:, :, cols] = mix.reshape(8, tokens, HEAD_DIM).astype(jnp.bfloat16)
            return 0

        def answer(n, _):
            to = (mine5 + n) % 8
            place = cross_mix.at[:, pl.ds(pl.multiple_of(mine5 * lot, HEAD_DIM), lot)]
            give(n == 0, cross_out.at[to], place, ANSWER, beside((to // 2) * 4 + y, to % 2))
            return 0

        wait_for(cross_in, t_recv.at[ASK])
        wait_for(text, t_recv.at[ROWS])
        lax.fori_loop(0, 5, head, 0)
        lax.fori_loop(0, 8, answer, 0)

    def attend(hs):
        def block(i, _):
            query = flat(q_in[hs, 0, pl.ds(i * group, group)])
            scores = [
                lax.dot_general(query, kv[m, hs, 0], (((1,), (1,)), ((), ())), preferred_element_type=jnp.float32)
                for m in range(STOPS)
            ]
            peaks = [jnp.max(s, axis=1, keepdims=True) - shut[m] for m, s in enumerate(scores)]
            peak = jnp.maximum(jnp.maximum(peaks[0], peaks[1]), peaks[2]) * SCORE
            weights = [jnp.exp2(s * SCORE - (peak + shut[m])) for m, s in enumerate(scores)]
            sums = sum(jnp.sum(w, axis=1, keepdims=True) for w in weights)
            mix = sum(
                jnp.dot(w.astype(jnp.bfloat16), kv[m, hs, 1], preferred_element_type=jnp.float32)
                for m, w in enumerate(weights)
            )
            mixed = mix / sums
            result[hs, pl.ds(i * group, group)] = mixed.reshape(group, tokens, HEAD_DIM).astype(jnp.bfloat16)

            def hand_back(n, _):
                s = i * group + n
                mine = jnp.logical_and(s == slot, home)
                where = self_mix.at[:, pl.ds(pl.multiple_of(my_col + hs * HEAD_DIM, HEAD_DIM), HEAD_DIM)]

                @pl.when(jnp.logical_not(mine))
                def _():
                    pltpu.make_async_remote_copy(
                        src_ref=result.at[hs, s],
                        dst_ref=where,
                        send_sem=o_send.at[hs],
                        recv_sem=o_recv,
                        device_id=(s // 2, e * COLUMNS + c, s % 2),
                        device_id_type=MESH,
                    ).start()

                @pl.when(mine)
                def _():
                    pltpu.make_async_copy(result.at[hs, s], where, o_recv).start()

                return 0

            lax.fori_loop(0, group, hand_back, 0)
            return 0

        def run():
            wait_for(q_in.at[hs], q_recv.at[hs])
            forward(hs, 1).wait_recv()
            lax.fori_loop(0, SOURCES // group, block, 0)

        per_slot(hs, run)

    attend(0)

    wait_for(text.at[pl.ds(0, RING - 1), 0], t_recv.at[UP])
    chunk = e * COLUMNS + c

    def send_text(n, _):
        to, row = (mine5 + n // 4) % 8, (y + n) % 4
        give(n == 0, column.at[:, to], text.at[chunk], ROWS, beside((to // 2) * 4 + row, to % 2))
        return 0

    lax.fori_loop(0, 32, send_text, 0)

    attend(1)
    attend(2)
    cross()

    for hs in (1, 2):
        sent(1, hs, 0)
        sent(1, hs, 1)
    wait_for(part.at[pl.ds(0, COLUMNS - 1)], t_send.at[PART])
    wait_for(other, t_send.at[SWAP])
    wait_for(cross_in.at[pl.ds(0, 7)], t_send.at[ASK])
    wait_for(cross_out.at[pl.ds(0, 7)], t_send.at[ANSWER])
    wait_for(text.at[pl.ds(0, 31)], t_send.at[ROWS])
    wait_for(text.at[pl.ds(0, RING - 1), 0], t_send.at[UP])
    for hs in range(SLOTS):

        def finish(hs=hs):
            forward(hs, 0).wait_send()
            forward(hs, 1).wait_send()

            @pl.when(home)
            def _():
                wait_for(result.at[hs, pl.ds(0, SOURCES - 1)], o_send.at[hs])

            @pl.when(jnp.logical_not(home))
            def _():
                wait_for(result.at[hs], o_send.at[hs])

        per_slot(hs, finish)
    wait_for(cross_mix, t_recv.at[ANSWER])
    wait_for(self_mix, o_recv)
    out_ref[...] = (self_mix[...].astype(jnp.float32) + cross_mix[...].astype(jnp.float32)).astype(jnp.bfloat16)


def body(
    queries,
    key_rows,
    value_rows,
    text_queries,
    prompt_embed,
    key_weight,
    value_weight,
    stop_count,
    prompt_length,
):
    tokens, width = queries.shape[1:]
    heads_here = key_weight.shape[1]
    text_rows = prompt_embed.shape[0] // COLUMNS
    dma = pltpu.SemaphoreType.DMA
    mixed = pl.pallas_call(
        kernel,
        out_shape=jax.ShapeDtypeStruct((tokens, width), jnp.bfloat16),
        in_specs=[pl.BlockSpec(memory_space=pltpu.HBM)] * 7
        + [pl.BlockSpec(memory_space=pltpu.SMEM)] * 2,
        out_specs=pl.BlockSpec(memory_space=pltpu.VMEM),
        scratch_shapes=[
            pltpu.VMEM((SLOTS, 2, SOURCES, tokens, HEAD_DIM), jnp.bfloat16),
            pltpu.VMEM((SLOTS, 1, SOURCES, tokens, HEAD_DIM), jnp.bfloat16),
            pltpu.VMEM((STOPS, SLOTS, 2, SOURCES * tokens, HEAD_DIM), jnp.bfloat16),
            pltpu.VMEM((COLUMNS, 2, text_rows, heads_here), jnp.float32),
            pltpu.VMEM((COLUMNS, 2, text_rows, heads_here), jnp.float32),
            pltpu.VMEM((2, text_rows, heads_here), jnp.float32),
            pltpu.VMEM((text_rows, heads_here), jnp.float32),
            pltpu.VMEM((text_rows, heads_here), jnp.bfloat16),
            pltpu.VMEM((2, 8, text_rows, heads_here), jnp.bfloat16),
            pltpu.VMEM((2 * COLUMNS, 2, text_rows, heads_here), jnp.bfloat16),
            pltpu.VMEM((SLOTS, SOURCES, tokens, HEAD_DIM), jnp.bfloat16),
            pltpu.VMEM((2, 8, 128), jnp.float32),
            pltpu.VMEM(prompt_embed.shape, jnp.bfloat16),
            pltpu.VMEM(key_weight.shape, jnp.bfloat16),
            pltpu.VMEM(value_weight.shape, jnp.bfloat16),
            pltpu.VMEM((8, tokens, heads_here), jnp.bfloat16),
            pltpu.VMEM((8, tokens, heads_here), jnp.bfloat16),
            pltpu.VMEM((tokens, width), jnp.bfloat16),
            pltpu.VMEM((tokens, width), jnp.bfloat16),
            dma((SLOTS,)),
            dma((SLOTS,)),
            dma((2, SLOTS, 2)),
            dma((2, SLOTS)),
            dma((2, SLOTS)),
            dma((SLOTS,)),
            dma,
            dma((7,)),
            dma((7,)),
            dma((3,)),
        ],
        compiler_params=pltpu.CompilerParams(
            collective_id=0, has_side_effects=True, vmem_limit_bytes=63 * 1024 * 1024
        ),
    )(
        queries[0],
        key_rows[0],
        value_rows[0],
        text_queries[0],
        prompt_embed,
        key_weight,
        value_weight,
        stop_count,
        prompt_length,
    )
    return mixed[None]


def solution(mesh):
    placed = (
        P("blk", ("head", "enc"), None),
        P("blk", ("head", "enc"), None),
        P("blk", ("head", "enc"), None),
        P("blk", ("head", "enc"), None),
        P("enc", "blk"),
        P("blk", "head"),
        P("blk", "head"),
        P("blk"),
        P(),
    )
    return jax.shard_map(
        body, mesh=mesh, in_specs=placed, out_specs=P("blk", ("head", "enc"), None), check_vma=False
    )
```

```python
import functools

import jax
import jax.numpy as jnp
from jax import lax
from jax.experimental import pallas as pl
from jax.experimental.pallas import tpu as pltpu
from jax.sharding import PartitionSpec as P

HEAD_DIM = 128
STOPS = 3
MESH = pl.DeviceIdType.MESH
COLUMNS = 16
RING = 16
SOURCES = 16
SLOTS = 3
SCORE = float(HEAD_DIM) ** -0.5 * 1.4426950408889634
OUT = 1.0e30
TRADE, PART, SWAP, ASK, UP, ROWS, ANSWER = range(7)


def kernel(
    q_ref, k_ref, v_ref, tq_ref, emb_hbm, wk_hbm, wv_hbm, stop_ref, plen_ref, out_ref,
    kv_in, q_in, kv, part, part_in, total, other, piece, column, text, result, stops, emb_ref, wk_ref, wv_ref,
    cross_in, cross_out, self_mix, cross_mix,
    kv_recv, q_recv, send, fwd_send, fwd_recv, o_send, o_recv, t_send, t_recv, w_sem,
):
    g = lax.axis_index("head")
    b = lax.axis_index("blk")
    e = lax.axis_index("enc")
    p = b // COLUMNS
    c = b % COLUMNS
    x, y = c // 4, c % 4
    z = p * 8 + g
    wide = z % 2 == 0
    home = e == p
    my_col = (z // 2) * 640 + jnp.where(wide, 0, 384)
    slot = g * 2 + e
    tokens = kv_in.shape[3]
    rows = SOURCES * tokens

    weights = [
        pltpu.make_async_copy(source, place, w_sem.at[i])
        for i, (source, place) in enumerate(((emb_hbm, emb_ref), (wk_hbm, wk_ref), (wv_hbm, wv_ref)))
    ]
    for copy in weights:
        copy.start()

    barrier = pltpu.get_barrier_semaphore()

    def greet(device):
        pl.semaphore_signal(barrier, inc=1, device_id=device, device_id_type=MESH)

    def at(height, core):
        return (height % 8, (height // 8) * COLUMNS + c, core)

    def beside(where, core):
        return (g, p * COLUMNS + where, core)

    def greet_column(n, _):
        height, core = n // 2, n % 2

        @pl.when(jnp.logical_or(height != z, core != e))
        def _():
            greet(at(height, core))

        return 0

    def greet_plane(n, _):
        greet(beside((c + n // 2) % COLUMNS, n % 2))
        return 0

    lax.fori_loop(0, 2 * RING, greet_column, 0)
    lax.fori_loop(2, 2 * COLUMNS, greet_plane, 0)
    pl.semaphore_wait(barrier, 61)

    def copy_to(source, place, kind, device):
        return pltpu.make_async_remote_copy(
            src_ref=source,
            dst_ref=place,
            send_sem=t_send.at[kind],
            recv_sem=t_recv.at[kind],
            device_id=device,
            device_id_type=MESH,
        )

    def give(mine, source, place, kind, device):
        @pl.when(jnp.logical_not(mine))
        def _():
            copy_to(source, place, kind, device).start()

        @pl.when(mine)
        def _():
            pltpu.make_async_copy(source, place, t_recv.at[kind]).start()

    def send_heads(kind, hs, half):
        refs, landing, recv = ((k_ref, v_ref), kv_in, kv_recv) if kind == 0 else ((q_ref,), q_in, q_recv)

        def one(n, _):
            m = jnp.where(n % 2 == 0, RING - 1 - n // 2, n // 2)
            t = (z + ((m + 1) // 2) * (2 * (m % 2) - 1) + RING) % RING
            col = pl.multiple_of((t // 2) * 640 + (t % 2) * 384 + hs * HEAD_DIM, HEAD_DIM)
            mine = jnp.logical_and(t == z, home)
            needed = t % 2 == 0 if hs == 2 else True

            @pl.when(jnp.logical_and(jnp.logical_not(mine), needed))
            def _():
                for i, ref in enumerate(refs):
                    pltpu.make_async_remote_copy(
                        src_ref=ref.at[:, pl.ds(col, HEAD_DIM)],
                        dst_ref=landing.at[hs, i, slot],
                        send_sem=send.at[kind, hs, half],
                        recv_sem=recv.at[hs],
                        device_id=at(t, p),
                        device_id_type=MESH,
                    ).start()

            @pl.when(jnp.logical_and(mine, needed))
            def _():
                for i, ref in enumerate(refs):
                    pltpu.make_async_copy(
                        ref.at[:, pl.ds(col, HEAD_DIM)], landing.at[hs, i, slot], recv.at[hs]
                    ).start()

            return 0

        lax.fori_loop(8 * half, 8 * half + 8, one, 0)

    def sent(kind, hs, half):
        landing = kv_in if kind == 0 else q_in
        count = 4 if hs == 2 else 8

        def left(copies):
            wait_for(landing.at[hs, :, pl.ds(0, copies)], send.at[kind, hs, half])

        if half == 1:
            left(count)
            return
        keeps = jnp.logical_and(home, wide) if hs == 2 else home

        @pl.when(keeps)
        def _():
            left(count - 1)

        @pl.when(jnp.logical_not(keeps))
        def _():
            left(count)

    def wait_for(ref, sem):
        pltpu.make_async_copy(ref, ref, sem).wait()

    def per_slot(hs, run):
        if hs == 2:
            pl.when(wide)(run)
        else:
            run()

    def forward(hs, m):
        next_c = (c + 1) % COLUMNS
        next_e = jnp.where(c == COLUMNS - 1, 1 - e, e)
        return pltpu.make_async_remote_copy(
            src_ref=kv.at[m, hs],
            dst_ref=kv.at[m + 1, hs],
            send_sem=fwd_send.at[m, hs],
            recv_sem=fwd_recv.at[m, hs],
            device_id=(g, p * COLUMNS + next_c, next_e),
            device_id_type=MESH,
        )

    def keys_arrive(hs):
        def run():
            wait_for(kv_in.at[hs], kv_recv.at[hs])
            for i in range(2):
                whole = kv_in[hs, i].astype(jnp.float32).reshape(rows, HEAD_DIM)
                kv[0, hs, i] = whole.astype(jnp.bfloat16)
            forward(hs, 0).start()

        per_slot(hs, run)

    def keys_pass(hs):
        def run():
            forward(hs, 0).wait_recv()
            forward(hs, 1).start()

        per_slot(hs, run)


    send_heads(0, 0, 0)
    send_heads(0, 0, 1)

    stops[0] = jnp.full((8, 128), stop_ref[0].astype(jnp.float32))
    trade = copy_to(stops.at[0], stops.at[1], TRADE, at((1 - p) * 8 + g, e))
    trade.start()

    for copy in weights:
        copy.wait()

    for i, w_ref in enumerate((wk_ref, wv_ref)):
        product = jnp.dot(emb_ref[...], w_ref[...], preferred_element_type=jnp.float32)
        part[:, i] = product.reshape(part.shape[0], part.shape[2], part.shape[3])

    def send_part(n, _):
        cc = (c + n) % COLUMNS
        copy_to(part.at[cc], part_in.at[c], PART, beside(cc, e)).start()
        return 0

    lax.fori_loop(1, COLUMNS, send_part, 0)
    part_in[c] = part[c]

    lot = 5 * HEAD_DIM
    mine5 = 2 * x + e

    def send_cross(n, _):
        to = (mine5 + n) % 8
        source = tq_ref.at[:, pl.ds(pl.multiple_of(to * lot, HEAD_DIM), lot)]
        give(n == 0, source, cross_in.at[mine5], ASK, beside((to // 2) * 4 + y, to % 2))
        return 0

    lax.fori_loop(0, 8, send_cross, 0)

    sent(0, 0, 0)
    send_heads(0, 1, 0)
    sent(0, 0, 1)
    send_heads(0, 1, 1)
    keys_arrive(0)

    wait_for(part_in.at[pl.ds(0, COLUMNS - 1)], t_recv.at[PART])
    total[...] = jnp.sum(part_in[...], axis=0)
    for n in range(5):
        cols = pl.ds(n * HEAD_DIM, HEAD_DIM)
        copy_to(total.at[1 - p, :, cols], other.at[:, cols], SWAP, at((1 - p) * 8 + g, e)).start()

    sent(0, 1, 0)
    send_heads(0, 2, 0)
    send_heads(0, 2, 1)
    keys_pass(0)

    wait_for(other, t_recv.at[SWAP])
    piece[...] = (total[p] + other[...]).astype(jnp.bfloat16)
    column[p, g] = piece[...]

    def send_up(n, _):
        copy_to(piece, column.at[p, g], UP, at((z + n) % RING, e)).start()
        return 0

    lax.fori_loop(1, RING, send_up, 0)

    sent(0, 1, 1)
    send_heads(1, 0, 0)
    send_heads(1, 0, 1)
    keys_arrive(1)

    sent(0, 2, 0)
    sent(0, 2, 1)
    send_heads(1, 1, 0)
    send_heads(1, 1, 1)
    keys_arrive(2)
    keys_pass(1)

    sent(1, 0, 0)
    sent(1, 0, 1)
    send_heads(1, 2, 0)
    send_heads(1, 2, 1)
    keys_pass(2)

    group = 4
    trade.wait()
    here = jnp.where(home, 1.0, 0.0)
    stop = stops[0, 0:1, 0:1] * here + stops[1, 0:1, 0:1] * (1.0 - here)
    shut = [jnp.where(m < stop, 0.0, OUT) for m in range(STOPS)]
    at_row = lax.broadcasted_iota(jnp.int32, (1, 2 * COLUMNS * 16), 1)
    live = at_row < plen_ref[0]

    def flat(values):
        return values.astype(jnp.float32).reshape(-1, HEAD_DIM).astype(jnp.bfloat16)

    def cross():
        def head(h, _):
            cols = pl.ds(pl.multiple_of(h * HEAD_DIM, HEAD_DIM), HEAD_DIM)
            query = flat(cross_in[:, :, cols])
            text_keys = text[:, 0, :, cols].reshape(512, HEAD_DIM)
            text_values = text[:, 1, :, cols].reshape(512, HEAD_DIM)
            scores = lax.dot_general(query, text_keys, (((1,), (1,)), ((), ())), preferred_element_type=jnp.float32)
            scores = jnp.where(live, scores, -OUT)
            weights = jnp.exp2((scores - jnp.max(scores, axis=1, keepdims=True)) * SCORE)
            mix = jnp.dot(weights.astype(jnp.bfloat16), text_values, preferred_element_type=jnp.float32)
            mix = mix / jnp.sum(weights, axis=1, keepdims=True)
            cross_out[:, :, cols] = mix.reshape(8, tokens, HEAD_DIM).astype(jnp.bfloat16)
            place = cross_mix.at[:, pl.ds(pl.multiple_of(mine5 * lot + h * HEAD_DIM, HEAD_DIM), HEAD_DIM)]

            def answer(n, _):
                to = (mine5 + n) % 8
                give(n == 0, cross_out.at[to, :, cols], place, ANSWER, beside((to // 2) * 4 + y, to % 2))
                return 0

            lax.fori_loop(0, 8, answer, 0)
            return 0

        wait_for(cross_in, t_recv.at[ASK])
        wait_for(text, t_recv.at[ROWS])
        lax.fori_loop(0, 5, head, 0)

    def attend(hs):
        def block(i, _):
            query = flat(q_in[hs, 0, pl.ds(i * group, group)])
            scores = [
                lax.dot_general(query, kv[m, hs, 0], (((1,), (1,)), ((), ())), preferred_element_type=jnp.float32)
                for m in range(STOPS)
            ]
            peaks = [jnp.max(s, axis=1, keepdims=True) - shut[m] for m, s in enumerate(scores)]
            peak = jnp.maximum(jnp.maximum(peaks[0], peaks[1]), peaks[2]) * SCORE
            weights = [jnp.exp2(s * SCORE - (peak + shut[m])) for m, s in enumerate(scores)]
            sums = sum(jnp.sum(w, axis=1, keepdims=True) for w in weights)
            mix = sum(
                jnp.dot(w.astype(jnp.bfloat16), kv[m, hs, 1], preferred_element_type=jnp.float32)
                for m, w in enumerate(weights)
            )
            mixed = mix / sums
            result[hs, pl.ds(i * group, group)] = mixed.reshape(group, tokens, HEAD_DIM).astype(jnp.bfloat16)

            def hand_back(n, _):
                s = i * group + n
                mine = jnp.logical_and(s == slot, home)
                where = self_mix.at[:, pl.ds(pl.multiple_of(my_col + hs * HEAD_DIM, HEAD_DIM), HEAD_DIM)]

                @pl.when(jnp.logical_not(mine))
                def _():
                    pltpu.make_async_remote_copy(
                        src_ref=result.at[hs, s],
                        dst_ref=where,
                        send_sem=o_send.at[hs],
                        recv_sem=o_recv,
                        device_id=(s // 2, e * COLUMNS + c, s % 2),
                        device_id_type=MESH,
                    ).start()

                @pl.when(mine)
                def _():
                    pltpu.make_async_copy(result.at[hs, s], where, o_recv).start()

                return 0

            lax.fori_loop(0, group, hand_back, 0)
            return 0

        def run():
            wait_for(q_in.at[hs], q_recv.at[hs])
            forward(hs, 1).wait_recv()
            lax.fori_loop(0, SOURCES // group, block, 0)

        per_slot(hs, run)

    attend(0)

    wait_for(text.at[pl.ds(0, RING - 1), 0], t_recv.at[UP])
    chunk = e * COLUMNS + c

    def send_text(n, _):
        to, row = (mine5 + n // 4) % 8, (y + n) % 4
        give(n == 0, column.at[:, to], text.at[chunk], ROWS, beside((to // 2) * 4 + row, to % 2))
        return 0

    lax.fori_loop(0, 32, send_text, 0)

    attend(1)
    attend(2)
    cross()

    for hs in (1, 2):
        sent(1, hs, 0)
        sent(1, hs, 1)
    wait_for(part.at[pl.ds(0, COLUMNS - 1)], t_send.at[PART])
    wait_for(other, t_send.at[SWAP])
    wait_for(cross_in.at[pl.ds(0, 7)], t_send.at[ASK])
    wait_for(cross_out.at[pl.ds(0, 7)], t_send.at[ANSWER])
    wait_for(text.at[pl.ds(0, 31)], t_send.at[ROWS])
    wait_for(text.at[pl.ds(0, RING - 1), 0], t_send.at[UP])
    for hs in range(SLOTS):

        def finish(hs=hs):
            forward(hs, 0).wait_send()
            forward(hs, 1).wait_send()

            @pl.when(home)
            def _():
                wait_for(result.at[hs, pl.ds(0, SOURCES - 1)], o_send.at[hs])

            @pl.when(jnp.logical_not(home))
            def _():
                wait_for(result.at[hs], o_send.at[hs])

        per_slot(hs, finish)
    wait_for(cross_mix, t_recv.at[ANSWER])
    wait_for(self_mix, o_recv)
    out_ref[...] = (self_mix[...].astype(jnp.float32) + cross_mix[...].astype(jnp.float32)).astype(jnp.bfloat16)


def body(
    queries,
    key_rows,
    value_rows,
    text_queries,
    prompt_embed,
    key_weight,
    value_weight,
    stop_count,
    prompt_length,
):
    tokens, width = queries.shape[1:]
    heads_here = key_weight.shape[1]
    text_rows = prompt_embed.shape[0] // COLUMNS
    dma = pltpu.SemaphoreType.DMA
    mixed = pl.pallas_call(
        kernel,
        out_shape=jax.ShapeDtypeStruct((tokens, width), jnp.bfloat16),
        in_specs=[pl.BlockSpec(memory_space=pltpu.HBM)] * 7
        + [pl.BlockSpec(memory_space=pltpu.SMEM)] * 2,
        out_specs=pl.BlockSpec(memory_space=pltpu.VMEM),
        scratch_shapes=[
            pltpu.VMEM((SLOTS, 2, SOURCES, tokens, HEAD_DIM), jnp.bfloat16),
            pltpu.VMEM((SLOTS, 1, SOURCES, tokens, HEAD_DIM), jnp.bfloat16),
            pltpu.VMEM((STOPS, SLOTS, 2, SOURCES * tokens, HEAD_DIM), jnp.bfloat16),
            pltpu.VMEM((COLUMNS, 2, text_rows, heads_here), jnp.float32),
            pltpu.VMEM((COLUMNS, 2, text_rows, heads_here), jnp.float32),
            pltpu.VMEM((2, text_rows, heads_here), jnp.float32),
            pltpu.VMEM((text_rows, heads_here), jnp.float32),
            pltpu.VMEM((text_rows, heads_here), jnp.bfloat16),
            pltpu.VMEM((2, 8, text_rows, heads_here), jnp.bfloat16),
            pltpu.VMEM((2 * COLUMNS, 2, text_rows, heads_here), jnp.bfloat16),
            pltpu.VMEM((SLOTS, SOURCES, tokens, HEAD_DIM), jnp.bfloat16),
            pltpu.VMEM((2, 8, 128), jnp.float32),
            pltpu.VMEM(prompt_embed.shape, jnp.bfloat16),
            pltpu.VMEM(key_weight.shape, jnp.bfloat16),
            pltpu.VMEM(value_weight.shape, jnp.bfloat16),
            pltpu.VMEM((8, tokens, heads_here), jnp.bfloat16),
            pltpu.VMEM((8, tokens, heads_here), jnp.bfloat16),
            pltpu.VMEM((tokens, width), jnp.bfloat16),
            pltpu.VMEM((tokens, width), jnp.bfloat16),
            dma((SLOTS,)),
            dma((SLOTS,)),
            dma((2, SLOTS, 2)),
            dma((2, SLOTS)),
            dma((2, SLOTS)),
            dma((SLOTS,)),
            dma,
            dma((7,)),
            dma((7,)),
            dma((3,)),
        ],
        compiler_params=pltpu.CompilerParams(
            collective_id=0, has_side_effects=True, vmem_limit_bytes=63 * 1024 * 1024
        ),
    )(
        queries[0],
        key_rows[0],
        value_rows[0],
        text_queries[0],
        prompt_embed,
        key_weight,
        value_weight,
        stop_count,
        prompt_length,
    )
    return mixed[None]


def solution(mesh):
    placed = (
        P("blk", ("head", "enc"), None),
        P("blk", ("head", "enc"), None),
        P("blk", ("head", "enc"), None),
        P("blk", ("head", "enc"), None),
        P("enc", "blk"),
        P("blk", "head"),
        P("blk", "head"),
        P("blk"),
        P(),
    )
    return jax.shard_map(
        body, mesh=mesh, in_specs=placed, out_specs=P("blk", ("head", "enc"), None), check_vma=False
    )
```

```python
import functools

import jax
import jax.numpy as jnp
from jax import lax
from jax.experimental import pallas as pl
from jax.experimental.pallas import tpu as pltpu
from jax.sharding import PartitionSpec as P

HEAD_DIM = 128
STOPS = 3
MESH = pl.DeviceIdType.MESH
COLUMNS = 16
RING = 16
SOURCES = 16
SLOTS = 3
SCORE = float(HEAD_DIM) ** -0.5 * 1.4426950408889634
OUT = 1.0e30
TRADE, PART, SWAP, ASK, UP, ROWS, ANSWER = range(7)


def kernel(
    q_ref, k_ref, v_ref, tq_ref, emb_hbm, wk_hbm, wv_hbm, stop_ref, plen_ref, out_ref,
    kv_in, q_in, kv, part, part_in, total, other, piece, column, text, result, stops, emb_ref, wk_ref, wv_ref,
    cross_in, cross_out, self_mix, cross_mix,
    kv_recv, q_recv, send, fwd_send, fwd_recv, o_send, o_recv, t_send, t_recv, w_sem,
):
    g = lax.axis_index("head")
    b = lax.axis_index("blk")
    e = lax.axis_index("enc")
    p = b // COLUMNS
    c = b % COLUMNS
    x, y = c // 4, c % 4
    z = p * 8 + g
    wide = z % 2 == 0
    home = e == p
    my_col = (z // 2) * 640 + jnp.where(wide, 0, 384)
    slot = g * 2 + e
    tokens = kv_in.shape[3]
    rows = SOURCES * tokens

    weights = [
        pltpu.make_async_copy(source, place, w_sem.at[i])
        for i, (source, place) in enumerate(((emb_hbm, emb_ref), (wk_hbm, wk_ref), (wv_hbm, wv_ref)))
    ]
    for copy in weights:
        copy.start()

    barrier = pltpu.get_barrier_semaphore()

    def greet(device):
        pl.semaphore_signal(barrier, inc=1, device_id=device, device_id_type=MESH)

    def at(height, core):
        return (height % 8, (height // 8) * COLUMNS + c, core)

    def beside(where, core):
        return (g, p * COLUMNS + where, core)

    def greet_column(n, _):
        height, core = n // 2, n % 2

        @pl.when(jnp.logical_or(height != z, core != e))
        def _():
            greet(at(height, core))

        return 0

    def greet_plane(n, _):
        greet(beside((c + n // 2) % COLUMNS, n % 2))
        return 0

    lax.fori_loop(0, 2 * RING, greet_column, 0)
    lax.fori_loop(2, 2 * COLUMNS, greet_plane, 0)
    pl.semaphore_wait(barrier, 61)

    def copy_to(source, place, kind, device):
        return pltpu.make_async_remote_copy(
            src_ref=source,
            dst_ref=place,
            send_sem=t_send.at[kind],
            recv_sem=t_recv.at[kind],
            device_id=device,
            device_id_type=MESH,
        )

    def give(mine, source, place, kind, device):
        @pl.when(jnp.logical_not(mine))
        def _():
            copy_to(source, place, kind, device).start()

        @pl.when(mine)
        def _():
            pltpu.make_async_copy(source, place, t_recv.at[kind]).start()

    def send_heads(kind, hs, half):
        refs, landing, recv = ((k_ref, v_ref), kv_in, kv_recv) if kind == 0 else ((q_ref,), q_in, q_recv)

        def one(n, _):
            m = jnp.where(n % 2 == 0, RING - 1 - n // 2, n // 2)
            t = (z + ((m + 1) // 2) * (2 * (m % 2) - 1) + RING) % RING
            col = pl.multiple_of((t // 2) * 640 + (t % 2) * 384 + hs * HEAD_DIM, HEAD_DIM)
            mine = jnp.logical_and(t == z, home)
            needed = t % 2 == 0 if hs == 2 else True

            @pl.when(jnp.logical_and(jnp.logical_not(mine), needed))
            def _():
                for i, ref in enumerate(refs):
                    pltpu.make_async_remote_copy(
                        src_ref=ref.at[:, pl.ds(col, HEAD_DIM)],
                        dst_ref=landing.at[hs, i, slot],
                        send_sem=send.at[kind, hs, half],
                        recv_sem=recv.at[hs],
                        device_id=at(t, p),
                        device_id_type=MESH,
                    ).start()

            @pl.when(jnp.logical_and(mine, needed))
            def _():
                for i, ref in enumerate(refs):
                    pltpu.make_async_copy(
                        ref.at[:, pl.ds(col, HEAD_DIM)], landing.at[hs, i, slot], recv.at[hs]
                    ).start()

            return 0

        lax.fori_loop(8 * half, 8 * half + 8, one, 0)

    def sent(kind, hs, half):
        landing = kv_in if kind == 0 else q_in
        count = 4 if hs == 2 else 8

        def left(copies):
            wait_for(landing.at[hs, :, pl.ds(0, copies)], send.at[kind, hs, half])

        if half == 1:
            left(count)
            return
        keeps = jnp.logical_and(home, wide) if hs == 2 else home

        @pl.when(keeps)
        def _():
            left(count - 1)

        @pl.when(jnp.logical_not(keeps))
        def _():
            left(count)

    def wait_for(ref, sem):
        pltpu.make_async_copy(ref, ref, sem).wait()

    def per_slot(hs, run):
        if hs == 2:
            pl.when(wide)(run)
        else:
            run()

    def forward(hs, m, i):
        next_c = (c + 1) % COLUMNS
        next_e = jnp.where(c == COLUMNS - 1, 1 - e, e)
        return pltpu.make_async_remote_copy(
            src_ref=kv.at[m, hs, i],
            dst_ref=kv.at[m + 1, hs, i],
            send_sem=fwd_send.at[m, hs, i],
            recv_sem=fwd_recv.at[m, hs, i],
            device_id=(g, p * COLUMNS + next_c, next_e),
            device_id_type=MESH,
        )

    def keys_arrive(hs):
        def run():
            wait_for(kv_in.at[hs], kv_recv.at[hs])
            for i in range(2):
                whole = kv_in[hs, i].astype(jnp.float32).reshape(rows, HEAD_DIM)
                kv[0, hs, i] = whole.astype(jnp.bfloat16)
                forward(hs, 0, i).start()

        per_slot(hs, run)

    def keys_pass(hs):
        def run():
            for i in range(2):
                forward(hs, 0, i).wait_recv()
                forward(hs, 1, i).start()

        per_slot(hs, run)


    send_heads(0, 0, 0)
    send_heads(0, 0, 1)

    stops[0] = jnp.full((8, 128), stop_ref[0].astype(jnp.float32))
    trade = copy_to(stops.at[0], stops.at[1], TRADE, at((1 - p) * 8 + g, e))
    trade.start()

    for copy in weights:
        copy.wait()

    for i, w_ref in enumerate((wk_ref, wv_ref)):
        product = jnp.dot(emb_ref[...], w_ref[...], preferred_element_type=jnp.float32)
        part[:, i] = product.reshape(part.shape[0], part.shape[2], part.shape[3])

    def send_part(n, _):
        cc = (c + n) % COLUMNS
        copy_to(part.at[cc], part_in.at[c], PART, beside(cc, e)).start()
        return 0

    lax.fori_loop(1, COLUMNS, send_part, 0)
    part_in[c] = part[c]

    lot = 5 * HEAD_DIM
    mine5 = 2 * x + e

    def send_cross(n, _):
        to = (mine5 + n) % 8
        source = tq_ref.at[:, pl.ds(pl.multiple_of(to * lot, HEAD_DIM), lot)]
        give(n == 0, source, cross_in.at[mine5], ASK, beside((to // 2) * 4 + y, to % 2))
        return 0

    lax.fori_loop(0, 8, send_cross, 0)

    sent(0, 0, 0)
    send_heads(0, 1, 0)
    sent(0, 0, 1)
    send_heads(0, 1, 1)
    keys_arrive(0)

    wait_for(part_in.at[pl.ds(0, COLUMNS - 1)], t_recv.at[PART])
    total[...] = jnp.sum(part_in[...], axis=0)
    for n in range(5):
        cols = pl.ds(n * HEAD_DIM, HEAD_DIM)
        copy_to(total.at[1 - p, :, cols], other.at[:, cols], SWAP, at((1 - p) * 8 + g, e)).start()

    sent(0, 1, 0)
    send_heads(0, 2, 0)
    send_heads(0, 2, 1)
    keys_pass(0)

    wait_for(other, t_recv.at[SWAP])
    piece[...] = (total[p] + other[...]).astype(jnp.bfloat16)
    column[p, g] = piece[...]

    def send_up(n, _):
        copy_to(piece, column.at[p, g], UP, at((z + n) % RING, e)).start()
        return 0

    lax.fori_loop(1, RING, send_up, 0)

    sent(0, 1, 1)
    send_heads(1, 0, 0)
    send_heads(1, 0, 1)
    keys_arrive(1)

    sent(0, 2, 0)
    sent(0, 2, 1)
    send_heads(1, 1, 0)
    send_heads(1, 1, 1)
    keys_arrive(2)
    keys_pass(1)

    sent(1, 0, 0)
    sent(1, 0, 1)
    send_heads(1, 2, 0)
    send_heads(1, 2, 1)
    keys_pass(2)

    group = 4
    trade.wait()
    here = jnp.where(home, 1.0, 0.0)
    stop = stops[0, 0:1, 0:1] * here + stops[1, 0:1, 0:1] * (1.0 - here)
    shut = [jnp.where(m < stop, 0.0, OUT) for m in range(STOPS)]
    at_row = lax.broadcasted_iota(jnp.int32, (1, 2 * COLUMNS * 16), 1)
    live = at_row < plen_ref[0]

    def flat(values):
        return values.astype(jnp.float32).reshape(-1, HEAD_DIM).astype(jnp.bfloat16)

    def cross():
        def head(h, _):
            cols = pl.ds(pl.multiple_of(h * HEAD_DIM, HEAD_DIM), HEAD_DIM)
            query = flat(cross_in[:, :, cols])
            text_keys = text[:, 0, :, cols].reshape(512, HEAD_DIM)
            text_values = text[:, 1, :, cols].reshape(512, HEAD_DIM)
            scores = lax.dot_general(query, text_keys, (((1,), (1,)), ((), ())), preferred_element_type=jnp.float32)
            scores = jnp.where(live, scores, -OUT)
            weights = jnp.exp2((scores - jnp.max(scores, axis=1, keepdims=True)) * SCORE)
            mix = jnp.dot(weights.astype(jnp.bfloat16), text_values, preferred_element_type=jnp.float32)
            mix = mix / jnp.sum(weights, axis=1, keepdims=True)
            cross_out[:, :, cols] = mix.reshape(8, tokens, HEAD_DIM).astype(jnp.bfloat16)
            place = cross_mix.at[:, pl.ds(pl.multiple_of(mine5 * lot + h * HEAD_DIM, HEAD_DIM), HEAD_DIM)]

            def answer(n, _):
                to = (mine5 + n) % 8
                give(n == 0, cross_out.at[to, :, cols], place, ANSWER, beside((to // 2) * 4 + y, to % 2))
                return 0

            lax.fori_loop(0, 8, answer, 0)
            return 0

        wait_for(cross_in, t_recv.at[ASK])
        wait_for(text, t_recv.at[ROWS])
        lax.fori_loop(0, 5, head, 0)

    def attend(hs):
        def block(i, _):
            query = flat(q_in[hs, 0, pl.ds(i * group, group)])
            scores = [
                lax.dot_general(query, kv[m, hs, 0], (((1,), (1,)), ((), ())), preferred_element_type=jnp.float32)
                for m in range(STOPS)
            ]
            peaks = [jnp.max(s, axis=1, keepdims=True) - shut[m] for m, s in enumerate(scores)]
            peak = jnp.maximum(jnp.maximum(peaks[0], peaks[1]), peaks[2]) * SCORE
            weights = [jnp.exp2(s * SCORE - (peak + shut[m])) for m, s in enumerate(scores)]
            sums = sum(jnp.sum(w, axis=1, keepdims=True) for w in weights)
            mix = sum(
                jnp.dot(w.astype(jnp.bfloat16), kv[m, hs, 1], preferred_element_type=jnp.float32)
                for m, w in enumerate(weights)
            )
            mixed = mix / sums
            result[hs, pl.ds(i * group, group)] = mixed.reshape(group, tokens, HEAD_DIM).astype(jnp.bfloat16)

            def hand_back(n, _):
                s = i * group + n
                mine = jnp.logical_and(s == slot, home)
                where = self_mix.at[:, pl.ds(pl.multiple_of(my_col + hs * HEAD_DIM, HEAD_DIM), HEAD_DIM)]

                @pl.when(jnp.logical_not(mine))
                def _():
                    pltpu.make_async_remote_copy(
                        src_ref=result.at[hs, s],
                        dst_ref=where,
                        send_sem=o_send.at[hs],
                        recv_sem=o_recv,
                        device_id=(s // 2, e * COLUMNS + c, s % 2),
                        device_id_type=MESH,
                    ).start()

                @pl.when(mine)
                def _():
                    pltpu.make_async_copy(result.at[hs, s], where, o_recv).start()

                return 0

            lax.fori_loop(0, group, hand_back, 0)
            return 0

        def run():
            wait_for(q_in.at[hs], q_recv.at[hs])
            for i in range(2):
                forward(hs, 1, i).wait_recv()
            lax.fori_loop(0, SOURCES // group, block, 0)

        per_slot(hs, run)

    attend(0)

    wait_for(text.at[pl.ds(0, RING - 1), 0], t_recv.at[UP])
    chunk = e * COLUMNS + c

    def send_text(n, _):
        to, row = (mine5 + n // 4) % 8, (y + n) % 4
        give(n == 0, column.at[:, to], text.at[chunk], ROWS, beside((to // 2) * 4 + row, to % 2))
        return 0

    lax.fori_loop(0, 32, send_text, 0)

    attend(1)
    attend(2)
    cross()

    for hs in (1, 2):
        sent(1, hs, 0)
        sent(1, hs, 1)
    wait_for(part.at[pl.ds(0, COLUMNS - 1)], t_send.at[PART])
    wait_for(other, t_send.at[SWAP])
    wait_for(cross_in.at[pl.ds(0, 7)], t_send.at[ASK])
    wait_for(cross_out.at[pl.ds(0, 7)], t_send.at[ANSWER])
    wait_for(text.at[pl.ds(0, 31)], t_send.at[ROWS])
    wait_for(text.at[pl.ds(0, RING - 1), 0], t_send.at[UP])
    for hs in range(SLOTS):

        def finish(hs=hs):
            for m in range(2):
                for i in range(2):
                    forward(hs, m, i).wait_send()

            @pl.when(home)
            def _():
                wait_for(result.at[hs, pl.ds(0, SOURCES - 1)], o_send.at[hs])

            @pl.when(jnp.logical_not(home))
            def _():
                wait_for(result.at[hs], o_send.at[hs])

        per_slot(hs, finish)
    wait_for(cross_mix, t_recv.at[ANSWER])
    wait_for(self_mix, o_recv)
    out_ref[...] = (self_mix[...].astype(jnp.float32) + cross_mix[...].astype(jnp.float32)).astype(jnp.bfloat16)


def body(
    queries,
    key_rows,
    value_rows,
    text_queries,
    prompt_embed,
    key_weight,
    value_weight,
    stop_count,
    prompt_length,
):
    tokens, width = queries.shape[1:]
    heads_here = key_weight.shape[1]
    text_rows = prompt_embed.shape[0] // COLUMNS
    dma = pltpu.SemaphoreType.DMA
    mixed = pl.pallas_call(
        kernel,
        out_shape=jax.ShapeDtypeStruct((tokens, width), jnp.bfloat16),
        in_specs=[pl.BlockSpec(memory_space=pltpu.HBM)] * 7
        + [pl.BlockSpec(memory_space=pltpu.SMEM)] * 2,
        out_specs=pl.BlockSpec(memory_space=pltpu.VMEM),
        scratch_shapes=[
            pltpu.VMEM((SLOTS, 2, SOURCES, tokens, HEAD_DIM), jnp.bfloat16),
            pltpu.VMEM((SLOTS, 1, SOURCES, tokens, HEAD_DIM), jnp.bfloat16),
            pltpu.VMEM((STOPS, SLOTS, 2, SOURCES * tokens, HEAD_DIM), jnp.bfloat16),
            pltpu.VMEM((COLUMNS, 2, text_rows, heads_here), jnp.float32),
            pltpu.VMEM((COLUMNS, 2, text_rows, heads_here), jnp.float32),
            pltpu.VMEM((2, text_rows, heads_here), jnp.float32),
            pltpu.VMEM((text_rows, heads_here), jnp.float32),
            pltpu.VMEM((text_rows, heads_here), jnp.bfloat16),
            pltpu.VMEM((2, 8, text_rows, heads_here), jnp.bfloat16),
            pltpu.VMEM((2 * COLUMNS, 2, text_rows, heads_here), jnp.bfloat16),
            pltpu.VMEM((SLOTS, SOURCES, tokens, HEAD_DIM), jnp.bfloat16),
            pltpu.VMEM((2, 8, 128), jnp.float32),
            pltpu.VMEM(prompt_embed.shape, jnp.bfloat16),
            pltpu.VMEM(key_weight.shape, jnp.bfloat16),
            pltpu.VMEM(value_weight.shape, jnp.bfloat16),
            pltpu.VMEM((8, tokens, heads_here), jnp.bfloat16),
            pltpu.VMEM((8, tokens, heads_here), jnp.bfloat16),
            pltpu.VMEM((tokens, width), jnp.bfloat16),
            pltpu.VMEM((tokens, width), jnp.bfloat16),
            dma((SLOTS,)),
            dma((SLOTS,)),
            dma((2, SLOTS, 2)),
            dma((2, SLOTS, 2)),
            dma((2, SLOTS, 2)),
            dma((SLOTS,)),
            dma,
            dma((7,)),
            dma((7,)),
            dma((3,)),
        ],
        compiler_params=pltpu.CompilerParams(
            collective_id=0, has_side_effects=True, vmem_limit_bytes=63 * 1024 * 1024
        ),
    )(
        queries[0],
        key_rows[0],
        value_rows[0],
        text_queries[0],
        prompt_embed,
        key_weight,
        value_weight,
        stop_count,
        prompt_length,
    )
    return mixed[None]


def solution(mesh):
    placed = (
        P("blk", ("head", "enc"), None),
        P("blk", ("head", "enc"), None),
        P("blk", ("head", "enc"), None),
        P("blk", ("head", "enc"), None),
        P("enc", "blk"),
        P("blk", "head"),
        P("blk", "head"),
        P("blk"),
        P(),
    )
    return jax.shard_map(
        body, mesh=mesh, in_specs=placed, out_specs=P("blk", ("head", "enc"), None), check_vma=False
    )
```
